32 devices in a mesh: tm: 16 (over z, x, core), quad: 2 (over y).
Axes of the slice: x: 2, y: 2, z: 4, core: 2. Of those that a mesh axis runs over, the one named last changes fastest.
Arguments:
- features: bfloat16 [16, 512, 192], P('tm', 'quad'), may hold values from -14 to 14
- w_query: bfloat16 [192, 192], replicated, may hold values from -1.25 to 1.25
- w_key: bfloat16 [192, 192], replicated, may hold values from -0.4375 to 0.4375
- w_value: bfloat16 [192, 192], replicated, may hold values from -0.4375 to 0.4375
- w_out: bfloat16 [192, 192], replicated, may hold values from -1.75 to 1.75
- block_offset: int32 [16, 4, 24], P('tm', 'quad'), may hold values from 0 to 2
- block_quad: int32 [16, 4, 24], P('tm', 'quad'), may hold values from 0 to 1
- block_tile: int32 [16, 4, 24], P('tm', 'quad'), may hold values from 0 to 1
- live_blocks: int32 [16, 4], P('tm', 'quad'), may hold values from 1 to 24, as said below
Outputs:
- mixed: bfloat16 [16, 512, 192], P('tm', 'quad')
The draws below stay inside these ranges and needn't reach their ends.
Inputs may be any that keep to these rules, and one draw needn't show every extreme that they name: `live_blocks`: some device has every one of its query tiles at 24 live blocks; on a quarter of the devices or so all tiles are at 24.
All inputs are finite; a program needn't handle non-finite values.
Results may differ from the reference program's by a relative error of at most 0.008.
The reference program's roundings to bfloat16 on the way (of `probs` and `attended`) count: a program that leaves them out, or rounds other values in their place, can miss the bound.
Values may be sent and summed in bfloat16 or wider, within the bound.
A program may use at most 64 MiB of HBM per device.

```python
import jax
import jax.numpy as jnp
from jax import lax

C = 192
HEADS = 6
TILE = 128
NB = 24
QT = 2
FRAMES = 16
CLIPS = 1
FRAME_TOK = 512
FRAME_TILES = 4
N_QUAD = 2


def draw_features(key, part):
    base = jax.random.normal(key, (FRAMES, FRAME_TOK, C), jnp.float32)
    return jnp.clip(base, -6.0, 6.0).astype(jnp.bfloat16)


def draw_live_blocks(key, part):
    first, second, third = jax.random.split(key, 3)
    base = jax.random.randint(first, (FRAMES, FRAME_TILES), 1, NB + 1)
    device = jnp.arange(FRAMES, dtype=jnp.int32)[:, None] * N_QUAD + jnp.arange(FRAME_TILES, dtype=jnp.int32)[None, :] // QT
    busy = jax.random.randint(second, (FRAMES * N_QUAD,), 0, 4) == 0
    chosen = jax.random.randint(third, (), 0, FRAMES * N_QUAD)
    full = jnp.take(busy, device) | (device == chosen)
    return jnp.where(full, NB, base).astype(jnp.int32)


def place_ends(entries, stream_key, low, largest):
    place = [jax.random.randint(jax.random.fold_in(stream_key, axis), (), 0, length) for axis, length in enumerate(entries.shape)]
    widest = entries.shape.index(max(entries.shape))
    beside = place[:widest] + [(place[widest] + 1) % entries.shape[widest]] + place[widest + 1:]
    return entries.at[tuple(place)].set(low).at[tuple(beside)].set(largest)


def bell_draw(stream_key, extent, deviation, bound, kind=jnp.bfloat16):
    array = jax.random.normal(stream_key, extent, jnp.float32) * deviation
    return jnp.minimum(jnp.maximum(array, -bound), bound).astype(kind)


def setup_inputs(seed: int = 0) -> dict:
    key_list = jax.random.split(jax.random.key(seed), 10)
    features = draw_features(jax.random.fold_in(key_list[9], 71), 0)
    w_query = bell_draw(key_list[1], (C, C), (C // 9) ** -0.5, 1.25)
    w_key = bell_draw(key_list[2], (C, C), C ** -0.5, 0.4375)
    w_value = bell_draw(key_list[3], (C, C), C ** -0.5, 0.4375)
    w_out = bell_draw(key_list[4], (C, C), (C // 16) ** -0.5, 1.75)
    block_offset = place_ends(jax.random.randint(key_list[5], (FRAMES, FRAME_TILES, NB), 0, 3), jax.random.fold_in(key_list[5], 1), 0, 2).astype(jnp.int32)
    block_quad = place_ends(jax.random.randint(key_list[6], (FRAMES, FRAME_TILES, NB), 0, N_QUAD), jax.random.fold_in(key_list[6], 1), 0, N_QUAD - 1).astype(jnp.int32)
    block_tile = place_ends(jax.random.randint(key_list[7], (FRAMES, FRAME_TILES, NB), 0, QT), jax.random.fold_in(key_list[7], 1), 0, QT - 1).astype(jnp.int32)
    live_blocks = draw_live_blocks(jax.random.fold_in(key_list[9], 71), 0)
    return {"features": features, "w_query": w_query, "w_key": w_key, "w_value": w_value, "w_out": w_out, "block_offset": block_offset, "block_quad": block_quad, "block_tile": block_tile, "live_blocks": live_blocks}


def reference(features, w_query, w_key, w_value, w_out, block_offset, block_quad, block_tile, live_blocks):
    frames, frame_tok, width = features.shape
    head_dim = width // HEADS
    flat = features.reshape(frames * frame_tok, width)
    query = (jnp.dot(flat, w_query, preferred_element_type=jnp.float32) * (head_dim ** -0.5)).astype(jnp.bfloat16)
    keys = jnp.dot(flat, w_key, preferred_element_type=jnp.float32).astype(jnp.bfloat16)
    values = jnp.dot(flat, w_value, preferred_element_type=jnp.float32).astype(jnp.bfloat16)
    frame_tiles = frame_tok // TILE
    kv_tiles = jnp.stack([keys, values]).reshape(2, frames * frame_tiles, TILE * width)
    frame_ids = jnp.arange(frames, dtype=jnp.int32)
    before = (frame_ids - CLIPS) % frames
    after = (frame_ids + CLIPS) % frames
    own = frame_ids[:, None, None]
    source = jnp.where(block_offset == 0, before[:, None, None], jnp.where(block_offset == 1, own, after[:, None, None]))
    global_ids = (source * frame_tiles + block_quad * QT + block_tile).astype(jnp.int32)
    global_ids = global_ids.reshape(frames * frame_tiles, NB)
    counts = live_blocks.reshape(frames * frame_tiles)
    query_tiles = query.reshape(frames * frame_tiles, TILE, width)

    def attend(packed):
        qtile, ids, count = packed
        taken = jnp.take(kv_tiles, ids, axis=1).reshape(2, NB * TILE, HEADS, head_dim)
        qheads = qtile.reshape(TILE, HEADS, head_dim).astype(jnp.float32)
        scores = jnp.einsum('qhd,khd->hqk', qheads, taken[0].astype(jnp.float32))
        live = (jnp.arange(NB * TILE, dtype=jnp.int32) // TILE) < count
        scores = jnp.where(live[None, None, :], scores, -jnp.inf)
        top = jnp.max(scores, axis=-1, keepdims=True)
        weights = jnp.exp(scores - top)
        total = jnp.sum(weights, axis=-1)
        probs = weights.astype(jnp.bfloat16)
        summed = jnp.einsum('hqk,khd->qhd', probs.astype(jnp.float32), taken[1].astype(jnp.float32))
        return (summed / total.T[:, :, None]).astype(jnp.bfloat16).reshape(TILE, width)

    attended = lax.map(attend, (query_tiles, global_ids, counts))
    mixed = jnp.dot(attended.reshape(frames * frame_tok, width), w_out, preferred_element_type=jnp.float32)
    return mixed.astype(jnp.bfloat16).reshape(frames, frame_tok, width)
```

```python
import functools

import jax
import jax.numpy as jnp
from jax import lax
from jax.experimental import pallas as pl
from jax.experimental.pallas import tpu as pltpu
from jax.sharding import PartitionSpec as P

HEADS = 6
TILE = 128
LOOP = 16
PARTS = 3
DEAD = -1e30
MESH = pl.DeviceIdType.MESH


def dot(a, b):
    return jnp.dot(a, b, preferred_element_type=jnp.float32)


def dot_nt(a, b):
    return lax.dot_general(a, b, (((1,), (1,)), ((), ())), preferred_element_type=jnp.float32)


def lanes(rows, columns):
    return lax.broadcasted_iota(jnp.int32, (rows, columns), 1)


def sublanes(rows, columns):
    return lax.broadcasted_iota(jnp.int32, (rows, columns), 0)


def kernel(
    pieces, frames, stride,
    feat_ref, wq_ref, wk_ref, wv_ref, offset_ref, quad_ref, tile_ref, live_ref,
    out_ref,
    window, wq, wk, wv, heads_q, bias, scores, peak, values, probs,
    load_sem, send_sem, recv_sem,
):
    tok, width = feat_ref.shape[1:]
    wide = heads_q.shape[-1]
    head_dim = width // HEADS
    tiles = tok // TILE
    frame, quad = lax.axis_index("tm"), lax.axis_index("quad")
    near, far = 2 - 2 * lax.rem(frame, 2), 2 * lax.rem(frame, 2)

    peers = []
    for rank, which in enumerate((far, 1, near)):
        for turn in range(pieces):
            if rank == 1 and turn == 0:
                continue
            there = lax.rem(frame + (which - 1) * stride + frames, frames)
            slot = (2 - which) * pieces + quad
            peers.append(({"tm": there, "quad": lax.rem(quad + turn, pieces)}, slot))

    barrier = pltpu.get_barrier_semaphore()
    for device, _ in peers:
        pl.semaphore_signal(barrier, inc=1, device_id=device, device_id_type=MESH)

    own = pieces + quad
    loads = [
        pltpu.make_async_copy(source, target, load_sem.at[n])
        for n, (source, target) in enumerate(
            ((feat_ref.at[0], window.at[own]), (wq_ref, wq), (wk_ref, wk), (wv_ref, wv))
        )
    ]
    for load in loads:
        load.start()
    pl.semaphore_wait(barrier, len(peers))
    sends = []
    for n, (device, slot) in enumerate(peers):
        send = pltpu.make_async_remote_copy(
            src_ref=feat_ref.at[0],
            dst_ref=window.at[slot],
            send_sem=send_sem.at[n],
            recv_sem=recv_sem.at[slot],
            device_id=device,
            device_id_type=MESH,
        )
        send.start()
        sends.append(send)

    rows = bias.shape[0]
    ids = offset_ref[0] * (pieces * tiles) + quad_ref[0] * tiles + tile_ref[0]
    blocks = ids.shape[1]
    lane = lanes(rows, wide)
    table = jnp.zeros((rows, wide), jnp.float32)
    for t in range(tiles):
        hit = (ids[t : t + 1] == sublanes(rows, blocks)) & (
            lanes(rows, blocks) < live_ref[:, t : t + 1]
        )
        count = jnp.sum(hit.astype(jnp.float32), axis=1, keepdims=True)
        rest = jnp.where(count > 0, jnp.log(jnp.maximum(count, 1.0)), DEAD)
        for part in range(PARTS):
            piece = rest.astype(jnp.bfloat16).astype(jnp.float32)
            table = table + jnp.where(lane == width + t * PARTS + part, piece, 0.0)
            rest = jnp.where(count > 0, rest - piece, 0.0)
    bias[...] = table
    peak[...] = jnp.full(peak.shape, -jnp.inf, jnp.float32)

    for load in loads:
        load.wait()
    place = (sublanes(width, wide) == lanes(width, wide)).astype(jnp.bfloat16)
    wide_q = dot(wq[...], place).astype(jnp.bfloat16)
    wide_k = dot(wk[...], place).astype(jnp.bfloat16)
    wide_v = dot(wv[...], place).astype(jnp.bfloat16)

    lane = lanes(tok, wide)
    query = (dot(window[own], wide_q) * head_dim ** (-0.5)).astype(jnp.bfloat16).astype(jnp.float32)
    row_tile = sublanes(tok, wide) // TILE
    start = width + row_tile * PARTS
    pick = ((lane >= start) & (lane < start + PARTS)).astype(jnp.float32)
    for h in range(HEADS):
        mine = (lane >= h * head_dim) & (lane < (h + 1) * head_dim)
        heads_q[h] = jnp.where(mine, query, pick).astype(jnp.bfloat16)
    ones = (lane >= width).astype(jnp.float32)

    def gather(step, slot):
        x = window[slot]
        column = pl.ds(pl.multiple_of(step * tok, tok), tok)
        keys = dot(x, wide_k)
        keys = jnp.concatenate(
            [
                keys[t * TILE : (t + 1) * TILE] + bias[pl.ds(slot * tiles + t, 1), :]
                for t in range(tiles)
            ],
            axis=0,
        ).astype(jnp.bfloat16)
        values[column, :] = (dot(x, wide_v) + ones).astype(jnp.bfloat16)
        for h in range(HEADS):
            s = dot_nt(heads_q[h], keys)
            scores[h, :, column] = s
            top = peak[h]
            for c in range(0, tok, TILE):
                top = jnp.maximum(top, s[:, c : c + TILE])
            peak[h] = top

    gather(0, own)

    def arrive(step, carry):
        turn = step // pieces
        which = jnp.where(turn == 0, 1, jnp.where(turn == 1, near, far))
        slot = which * pieces + lax.rem(quad + lax.rem(step, pieces), pieces)
        pltpu.make_async_copy(feat_ref.at[0], window.at[slot], recv_sem.at[slot]).wait()
        gather(step, slot)
        return carry

    lax.fori_loop(1, 3 * pieces, arrive, 0)

    keys_all = values.shape[0]
    total = jnp.zeros((tok, wide), jnp.float32)
    summed = jnp.zeros((tok, wide), jnp.float32)
    for h in range(HEADS):
        top = jnp.max(peak[h], axis=1, keepdims=True)
        for c in range(0, keys_all, tok):
            probs[h % 2, :, c : c + tok] = jnp.exp(scores[h, :, c : c + tok] - top).astype(jnp.bfloat16)
        o = dot(probs[h % 2], values[...])
        mine = (lane >= h * head_dim) & (lane < (h + 1) * head_dim)
        total = jnp.where(mine, o[:, width : width + 1], total)
        summed = jnp.where(mine, o, summed)
    out_ref[...] = (summed[:, :width] / total[:, :width]).astype(jnp.bfloat16)
    for send in sends:
        send.wait_send()


def body(
    features, w_query, w_key, w_value, w_out, block_offset, block_quad, block_tile, live_blocks
):
    tok, width = features.shape[1:]
    tiles = tok // TILE
    pieces, frames = lax.axis_size("quad"), lax.axis_size("tm")
    stride = frames // LOOP
    slots = 3 * pieces
    wide = -(-(width + PARTS * tiles) // 128) * 128
    keys = slots * tok
    rows = -(-slots * tiles // 8) * 8
    hbm = pl.BlockSpec(memory_space=pl.ANY)
    vmem = pl.BlockSpec(memory_space=pltpu.VMEM)
    big = HEADS * tok * keys * 4 + keys * wide * 2 + 2 * tok * keys * 2 + slots * tok * wide * 2
    attended = pl.pallas_call(
        functools.partial(kernel, pieces, frames, stride),
        out_shape=jax.ShapeDtypeStruct((tok, width), jnp.bfloat16),
        in_specs=[hbm] * 4 + [vmem] * 4,
        out_specs=vmem,
        scratch_shapes=[
            pltpu.VMEM((slots, tok, width), jnp.bfloat16),
            pltpu.VMEM((width, width), jnp.bfloat16),
            pltpu.VMEM((width, width), jnp.bfloat16),
            pltpu.VMEM((width, width), jnp.bfloat16),
            pltpu.VMEM((HEADS, tok, wide), jnp.bfloat16),
            pltpu.VMEM((rows, wide), jnp.float32),
            pltpu.VMEM((HEADS, tok, keys), jnp.float32),
            pltpu.VMEM((HEADS, tok, TILE), jnp.float32),
            pltpu.VMEM((keys, wide), jnp.bfloat16),
            pltpu.VMEM((2, tok, keys), jnp.bfloat16),
            pltpu.SemaphoreType.DMA((4,)),
            pltpu.SemaphoreType.DMA((slots - 1,)),
            pltpu.SemaphoreType.DMA((slots,)),
        ],
        compiler_params=pltpu.CompilerParams(
            collective_id=0, has_side_effects=True, vmem_limit_bytes=big + (8 << 20)
        ),
    )(features, w_query, w_key, w_value, block_offset, block_quad, block_tile, live_blocks)
    return jnp.dot(attended, w_out, preferred_element_type=jnp.float32).astype(jnp.bfloat16)[None]


def solution(mesh):
    listed = P("tm", "quad", None)
    return jax.shard_map(
        body,
        mesh=mesh,
        in_specs=(listed, P(), P(), P(), P(), listed, listed, listed, P("tm", "quad")),
        out_specs=listed,
        check_vma=False,
    )
```

```python
import functools

import jax
import jax.numpy as jnp
from jax import lax
from jax.experimental import pallas as pl
from jax.experimental.pallas import tpu as pltpu
from jax.sharding import PartitionSpec as P

HEADS = 6
TILE = 128
LOOP = 16
FAR = 1e30
MESH = pl.DeviceIdType.MESH


def dot(a, b):
    return jnp.dot(a, b, preferred_element_type=jnp.float32)


def lanes(rows, columns):
    return lax.broadcasted_iota(jnp.int32, (rows, columns), 1)


def sublanes(rows, columns):
    return lax.broadcasted_iota(jnp.int32, (rows, columns), 0)


def kernel(
    pieces, frames, stride,
    feat_ref, wq_ref, wk_ref, wv_ref, offset_ref, quad_ref, tile_ref, live_ref,
    out_ref,
    window, wq, wk, wv, offset, quads, places, live,
    queries, times, scores, peak, values,
    load_sem, send_sem, recv_sem,
):
    width, tok = feat_ref.shape
    head_dim = width // HEADS
    tiles = tok // TILE
    slots = 3 * pieces
    frame, quad = lax.axis_index("tm"), lax.axis_index("quad")
    near, far = 2 - 2 * lax.rem(frame, 2), 2 * lax.rem(frame, 2)
    own = pieces + quad

    peers = []
    for rank, which in enumerate((far, 1, near)):
        for turn in range(pieces):
            if rank == 1 and turn == 0:
                continue
            there = lax.rem(frame + (which - 1) * stride + frames, frames)
            slot = (2 - which) * pieces + quad
            peers.append(({"tm": there, "quad": lax.rem(quad + turn, pieces)}, slot))

    barrier = pltpu.get_barrier_semaphore()
    for device, _ in peers:
        pl.semaphore_signal(barrier, inc=1, device_id=device, device_id_type=MESH)

    pairs = (
        (wq_ref, wq), (feat_ref, window.at[own]), (wk_ref, wk), (wv_ref, wv),
        (offset_ref, offset), (quad_ref, quads), (tile_ref, places), (live_ref, live),
    )
    loads = [
        pltpu.make_async_copy(source, target, load_sem.at[n])
        for n, (source, target) in enumerate(pairs)
    ]
    for load in loads:
        load.start()
    pl.semaphore_wait(barrier, len(peers))
    sends = []
    for n, (device, slot) in enumerate(peers):
        send = pltpu.make_async_remote_copy(
            src_ref=feat_ref,
            dst_ref=window.at[slot],
            send_sem=send_sem.at[n],
            recv_sem=recv_sem.at[slot],
            device_id=device,
            device_id_type=MESH,
        )
        send.start()
        sends.append(send)
    for load in loads:
        load.wait()

    rows = times.shape[0]
    ids = offset[0] * (pieces * tiles) + quads[0] * tiles + places[0]
    blocks = ids.shape[1]
    query_tile = lanes(rows, tok) // TILE
    table = jnp.zeros((rows, tok), jnp.float32)
    for t in range(tiles):
        hit = (ids[t : t + 1] == sublanes(rows, blocks)) & (
            lanes(rows, blocks) < live[:, t : t + 1]
        )
        count = jnp.sum(hit.astype(jnp.float32), axis=1, keepdims=True)
        table = jnp.where(query_tile == t, count, table)
    times[...] = table
    peak[...] = jnp.full(peak.shape, -jnp.inf, jnp.float32)

    turned_q, turned_v = wq[...].T, wv[...].T
    query = (dot(turned_q, window[own]) * head_dim ** (-0.5)).astype(jnp.bfloat16)
    head = sublanes(width, tok) // head_dim
    for h in range(HEADS):
        queries[h] = jnp.where(head == h, query, jnp.zeros_like(query))
    key_tile = lanes(width, tok) // TILE

    def gather(slot):
        x = window[slot]
        keys = dot(x.T, wk[...]).astype(jnp.bfloat16)
        value = dot(turned_v, x).astype(jnp.bfloat16)
        for j in range(tiles):
            values[slot, j] = jnp.where(key_tile == j, value, jnp.zeros_like(value))
        used = [times[pl.ds(slot * tiles + j, 1), :] > 0 for j in range(tiles)]
        for h in range(HEADS):
            s = dot(keys, queries[h])
            scores[slot, h] = s
            top = peak[h]
            for j in range(tiles):
                part = s[j * TILE : (j + 1) * TILE].reshape(TILE // 8, 8, tok).max(axis=0)
                top = jnp.maximum(top, jnp.where(used[j], part, -jnp.inf))
            peak[h] = top

    gather(own)

    def arrive(step, carry):
        turn = step // pieces
        which = jnp.where(turn == 0, 1, jnp.where(turn == 1, near, far))
        slot = which * pieces + lax.rem(quad + lax.rem(step, pieces), pieces)
        pltpu.make_async_copy(feat_ref, window.at[slot], recv_sem.at[slot]).wait()
        gather(slot)
        return carry

    lax.fori_loop(1, slots, arrive, 0)

    for h in range(HEADS):
        top = jnp.max(peak[h], axis=0, keepdims=True)
        total = jnp.zeros((8, tok), jnp.float32)
        summed = jnp.zeros((head_dim, tok), jnp.float32)
        span = slice(h * head_dim, (h + 1) * head_dim)
        for slot in range(slots):
            probs, often = [], []
            for j in range(tiles):
                u = slot * tiles + j
                many = times[u : u + 1, :]
                shift = jnp.where(many > 0, top, FAR)
                w = jnp.exp(scores[slot, h, j * TILE : (j + 1) * TILE] - shift)
                total = total + many * w.reshape(TILE // 8, 8, tok).sum(axis=0)
                probs.append(w.astype(jnp.bfloat16))
                often.append(many)
            left = jnp.concatenate([values[slot, j, span] for j in range(tiles)], axis=0)
            o = dot(left, jnp.concatenate(probs, axis=0))
            for j in range(tiles):
                summed = summed + often[j] * o[j * head_dim : (j + 1) * head_dim]
        total = jnp.sum(total, axis=0, keepdims=True)
        out_ref[span, :] = (summed / total).astype(jnp.bfloat16)
    for send in sends:
        send.wait_send()


def body(
    features, w_query, w_key, w_value, w_out, block_offset, block_quad, block_tile, live_blocks
):
    tok, width = features.shape[1:]
    tiles = tok // TILE
    pieces, frames = lax.axis_size("quad"), lax.axis_size("tm")
    stride = frames // LOOP
    slots = 3 * pieces
    rows = -(-slots * tiles // 8) * 8
    listed = block_offset.shape
    hbm = pl.BlockSpec(memory_space=pltpu.HBM)
    vmem = pl.BlockSpec(memory_space=pltpu.VMEM)
    weights = pltpu.VMEM((width, width), jnp.bfloat16)
    attended = pl.pallas_call(
        functools.partial(kernel, pieces, frames, stride),
        out_shape=jax.ShapeDtypeStruct((width, tok), jnp.bfloat16),
        in_specs=[hbm] * 8,
        out_specs=vmem,
        scratch_shapes=[
            pltpu.VMEM((slots, width, tok), jnp.bfloat16),
            weights,
            weights,
            weights,
            pltpu.VMEM(listed, jnp.int32),
            pltpu.VMEM(listed, jnp.int32),
            pltpu.VMEM(listed, jnp.int32),
            pltpu.VMEM(live_blocks.shape, jnp.int32),
            pltpu.VMEM((HEADS, width, tok), jnp.bfloat16),
            pltpu.VMEM((rows, tok), jnp.float32),
            pltpu.VMEM((slots, HEADS, tok, tok), jnp.float32),
            pltpu.VMEM((HEADS, 8, tok), jnp.float32),
            pltpu.VMEM((slots, tiles, width, tok), jnp.bfloat16),
            pltpu.SemaphoreType.DMA((8,)),
            pltpu.SemaphoreType.DMA((slots - 1,)),
            pltpu.SemaphoreType.DMA((slots,)),
        ],
        compiler_params=pltpu.CompilerParams(
            collective_id=0, has_side_effects=True, vmem_limit_bytes=60 << 20
        ),
    )(features[0].T, w_query, w_key, w_value, block_offset, block_quad, block_tile, live_blocks)
    mixed = lax.dot_general(
        w_out, attended, (((0,), (0,)), ((), ())), preferred_element_type=jnp.float32
    )
    return mixed.astype(jnp.bfloat16).T[None]


def solution(mesh):
    listed = P("tm", "quad", None)
    return jax.shard_map(
        body,
        mesh=mesh,
        in_specs=(listed, P(), P(), P(), P(), listed, listed, listed, P("tm", "quad")),
        out_specs=listed,
        check_vma=False,
    )
```

```python
import functools

import jax
import jax.numpy as jnp
from jax import lax
from jax.experimental import pallas as pl
from jax.experimental.pallas import tpu as pltpu
from jax.sharding import PartitionSpec as P

HEADS = 6
TILE = 128
LOOP = 16
FAR = 1e30
MESH = pl.DeviceIdType.MESH


def dot(a, b):
    return jnp.dot(a, b, preferred_element_type=jnp.float32)


def lanes(rows, columns):
    return lax.broadcasted_iota(jnp.int32, (rows, columns), 1)


def sublanes(rows, columns):
    return lax.broadcasted_iota(jnp.int32, (rows, columns), 0)


def kernel(
    pieces, frames, stride,
    feat_ref, wq_ref, wk_ref, wv_ref, wo_ref, offset_ref, quad_ref, tile_ref, live_ref,
    out_ref,
    window, wq, wk, wv, wo, attended, offset, quads, places, live,
    queries, times, scores, peak, values,
    load_sem, send_sem, recv_sem,
):
    width, tok = feat_ref.shape
    head_dim = width // HEADS
    tiles = tok // TILE
    slots = 3 * pieces
    frame, quad = lax.axis_index("tm"), lax.axis_index("quad")
    near, far = 2 - 2 * lax.rem(frame, 2), 2 * lax.rem(frame, 2)
    own = pieces + quad

    paired = pieces == 2 and stride == 1
    across = 1 - quad
    behind, beyond = (lax.rem(frame + (w - 1) * stride + frames, frames) for w in (near, far))
    peers = []
    if paired:
        peers.append(({"tm": frame, "quad": across}, own))
        peers.append(({"tm": beyond, "quad": quad}, (2 - far) * pieces + quad))
        peers.append(({"tm": behind, "quad": quad}, (2 - near) * pieces + quad))
    for rank, which in enumerate((far, 1, near)):
        for turn in range(pieces):
            if paired or (rank == 1 and turn == 0):
                continue
            there = lax.rem(frame + (which - 1) * stride + frames, frames)
            slot = (2 - which) * pieces + quad
            peers.append(({"tm": there, "quad": lax.rem(quad + turn, pieces)}, slot))

    barrier = pltpu.get_barrier_semaphore()
    for device, _ in peers:
        pl.semaphore_signal(barrier, inc=1, device_id=device, device_id_type=MESH)

    pairs = (
        (wq_ref, wq), (feat_ref, window.at[own]), (wk_ref, wk), (wv_ref, wv),
        (offset_ref, offset), (quad_ref, quads), (tile_ref, places), (live_ref, live),
        (wo_ref, wo),
    )
    loads = [
        pltpu.make_async_copy(source, target, load_sem.at[n])
        for n, (source, target) in enumerate(pairs)
    ]
    for load in loads:
        load.start()
    pl.semaphore_wait(barrier, len(peers))
    sends = []

    def launch(source, device, slot):
        send = pltpu.make_async_remote_copy(
            src_ref=source,
            dst_ref=window.at[slot],
            send_sem=send_sem.at[len(sends)],
            recv_sem=recv_sem.at[slot],
            device_id=device,
            device_id_type=MESH,
        )
        send.start()
        sends.append(send)

    for device, slot in peers:
        launch(feat_ref, device, slot)
    for load in loads:
        load.wait()

    rows = times.shape[0]
    ids = offset[0] * (pieces * tiles) + quads[0] * tiles + places[0]
    blocks = ids.shape[1]
    query_tile = lanes(rows, tok) // TILE
    table = jnp.zeros((rows, tok), jnp.float32)
    for t in range(tiles):
        hit = (ids[t : t + 1] == sublanes(rows, blocks)) & (
            lanes(rows, blocks) < live[:, t : t + 1]
        )
        count = jnp.sum(hit.astype(jnp.float32), axis=1, keepdims=True)
        table = jnp.where(query_tile == t, count, table)
    times[...] = table
    peak[...] = jnp.full(peak.shape, -jnp.inf, jnp.float32)

    turned_q, turned_v = wq[...].T, wv[...].T
    query = (dot(turned_q, window[own]) * head_dim ** (-0.5)).astype(jnp.bfloat16)
    head = sublanes(width, tok) // head_dim
    for h in range(HEADS):
        queries[h] = jnp.where(head == h, query, jnp.zeros_like(query))
    key_tile = lanes(width, tok) // TILE

    def gather(slot):
        x = window[slot]
        keys = dot(x.T, wk[...]).astype(jnp.bfloat16)
        value = dot(turned_v, x).astype(jnp.bfloat16)
        for j in range(tiles):
            values[slot, j] = jnp.where(key_tile == j, value, jnp.zeros_like(value))
        used = [times[pl.ds(slot * tiles + j, 1), :] > 0 for j in range(tiles)]
        for h in range(HEADS):
            s = dot(keys, queries[h])
            scores[slot, h] = s
            top = peak[h]
            for j in range(tiles):
                part = s[j * TILE : (j + 1) * TILE].reshape(TILE // 8, 8, tok).max(axis=0)
                top = jnp.maximum(top, jnp.where(used[j], part, -jnp.inf))
            peak[h] = top

    gather(own)

    def landed(slot):
        pltpu.make_async_copy(feat_ref, window.at[slot], recv_sem.at[slot]).wait()

    if paired:
        facing, distant = pieces + across, far * pieces + quad
        landed(facing)
        launch(window.at[facing], {"tm": behind, "quad": quad}, (2 - near) * pieces + across)
        landed(distant)
        row = lax.rem(frame // 2 + lax.rem(frame, 2), 2)
        launch(
            window.at[jnp.where(row == 1, distant, facing)],
            {
                "tm": jnp.where(row == 1, frame, beyond),
                "quad": jnp.where(row == 1, across, quad),
            },
            jnp.where(row == 1, distant, (2 - far) * pieces + across),
        )
        landed(near * pieces + quad)

        def early(step, carry):
            which = jnp.where(step == 0, 1, jnp.where(step == 1, near, far))
            gather(which * pieces + jnp.where(step == 0, across, quad))
            return carry

        def late(step, carry):
            slot = jnp.where(step == 0, near, far) * pieces + across
            landed(slot)
            gather(slot)
            return carry

        lax.fori_loop(0, 3, early, 0)
        lax.fori_loop(0, 2, late, 0)
    else:

        def arrive(step, carry):
            turn = step // pieces
            which = jnp.where(turn == 0, 1, jnp.where(turn == 1, near, far))
            slot = which * pieces + lax.rem(quad + lax.rem(step, pieces), pieces)
            landed(slot)
            gather(slot)
            return carry

        lax.fori_loop(1, slots, arrive, 0)

    for h in range(HEADS):
        top = jnp.max(peak[h], axis=0, keepdims=True)
        total = jnp.zeros((8, tok), jnp.float32)
        summed = jnp.zeros((head_dim, tok), jnp.float32)
        span = slice(h * head_dim, (h + 1) * head_dim)
        for slot in range(slots):
            probs, often = [], []
            for j in range(tiles):
                u = slot * tiles + j
                many = times[u : u + 1, :]
                shift = jnp.where(many > 0, top, FAR)
                w = jnp.exp(scores[slot, h, j * TILE : (j + 1) * TILE] - shift)
                total = total + many * w.reshape(TILE // 8, 8, tok).sum(axis=0)
                probs.append(w.astype(jnp.bfloat16))
                often.append(many)
            left = jnp.concatenate([values[slot, j, span] for j in range(tiles)], axis=0)
            o = dot(left, jnp.concatenate(probs, axis=0))
            for j in range(tiles):
                summed = summed + often[j] * o[j * head_dim : (j + 1) * head_dim]
        total = jnp.sum(total, axis=0, keepdims=True)
        attended[span, :] = (summed / total).astype(jnp.bfloat16)
    out_ref[...] = dot(wo[...].T, attended[...]).astype(jnp.bfloat16)
    for send in sends:
        send.wait_send()


def body(
    features, w_query, w_key, w_value, w_out, block_offset, block_quad, block_tile, live_blocks
):
    tok, width = features.shape[1:]
    tiles = tok // TILE
    pieces, frames = lax.axis_size("quad"), lax.axis_size("tm")
    stride = frames // LOOP
    slots = 3 * pieces
    rows = -(-slots * tiles // 8) * 8
    listed = block_offset.shape
    hbm = pl.BlockSpec(memory_space=pltpu.HBM)
    vmem = pl.BlockSpec(memory_space=pltpu.VMEM)
    weights = pltpu.VMEM((width, width), jnp.bfloat16)
    mixed = pl.pallas_call(
        functools.partial(kernel, pieces, frames, stride),
        out_shape=jax.ShapeDtypeStruct((width, tok), jnp.bfloat16),
        in_specs=[hbm] * 9,
        out_specs=vmem,
        scratch_shapes=[
            pltpu.VMEM((slots, width, tok), jnp.bfloat16),
            weights,
            weights,
            weights,
            weights,
            pltpu.VMEM((width, tok), jnp.bfloat16),
            pltpu.VMEM(listed, jnp.int32),
            pltpu.VMEM(listed, jnp.int32),
            pltpu.VMEM(listed, jnp.int32),
            pltpu.VMEM(live_blocks.shape, jnp.int32),
            pltpu.VMEM((HEADS, width, tok), jnp.bfloat16),
            pltpu.VMEM((rows, tok), jnp.float32),
            pltpu.VMEM((slots, HEADS, tok, tok), jnp.float32),
            pltpu.VMEM((HEADS, 8, tok), jnp.float32),
            pltpu.VMEM((slots, tiles, width, tok), jnp.bfloat16),
            pltpu.SemaphoreType.DMA((9,)),
            pltpu.SemaphoreType.DMA((slots - 1,)),
            pltpu.SemaphoreType.DMA((slots,)),
        ],
        compiler_params=pltpu.CompilerParams(
            collective_id=0, has_side_effects=True, vmem_limit_bytes=60 << 20
        ),
    )(features[0].T, w_query, w_key, w_value, w_out, block_offset, block_quad, block_tile, live_blocks)
    return mixed.T[None]


def solution(mesh):
    listed = P("tm", "quad", None)
    return jax.shard_map(
        body,
        mesh=mesh,
        in_specs=(listed, P(), P(), P(), P(), listed, listed, listed, P("tm", "quad")),
        out_specs=listed,
        check_vma=False,
    )
```

```python
import functools

import jax
import jax.numpy as jnp
from jax import lax
from jax.experimental import pallas as pl
from jax.experimental.pallas import tpu as pltpu
from jax.sharding import PartitionSpec as P

HEADS = 6
TILE = 128
LOOP = 16
FAR = 1e30
MESH = pl.DeviceIdType.MESH


def dot(a, b):
    return jnp.dot(a, b, preferred_element_type=jnp.float32)


def lanes(rows, columns):
    return lax.broadcasted_iota(jnp.int32, (rows, columns), 1)


def sublanes(rows, columns):
    return lax.broadcasted_iota(jnp.int32, (rows, columns), 0)


def kernel(
    pieces, frames, stride,
    feat_ref, wq_ref, wk_ref, wv_ref, wo_ref, offset_ref, quad_ref, tile_ref, live_ref,
    out_ref,
    window, wq, wk, wv, wo, attended, offset, quads, places, live,
    queries, times, scores, peak, values,
    load_sem, send_sem, recv_sem,
):
    width, tok = feat_ref.shape
    head_dim = width // HEADS
    tiles = tok // TILE
    slots = 3 * pieces
    frame, quad = lax.axis_index("tm"), lax.axis_index("quad")
    near, far = 2 - 2 * lax.rem(frame, 2), 2 * lax.rem(frame, 2)
    own = pieces + quad

    peers = []
    for rank, which in enumerate((far, 1, near)):
        for turn in range(pieces):
            if rank == 1 and turn == 0:
                continue
            there = lax.rem(frame + (which - 1) * stride + frames, frames)
            slot = (2 - which) * pieces + quad
            peers.append(({"tm": there, "quad": lax.rem(quad + turn, pieces)}, slot))

    barrier = pltpu.get_barrier_semaphore()
    for device, _ in peers:
        pl.semaphore_signal(barrier, inc=1, device_id=device, device_id_type=MESH)

    pairs = (
        (wq_ref, wq), (feat_ref, window.at[own]), (wk_ref, wk), (wv_ref, wv),
        (offset_ref, offset), (quad_ref, quads), (tile_ref, places), (live_ref, live),
        (wo_ref, wo),
    )
    loads = [
        pltpu.make_async_copy(source, target, load_sem.at[n])
        for n, (source, target) in enumerate(pairs)
    ]
    for load in loads:
        load.start()
    for load in loads:
        load.wait()

    rows = times.shape[0]
    ids = offset[0] * (pieces * tiles) + quads[0] * tiles + places[0]
    blocks = ids.shape[1]
    query_tile = lanes(rows, tok) // TILE
    table = jnp.zeros((rows, tok), jnp.float32)
    for t in range(tiles):
        hit = (ids[t : t + 1] == sublanes(rows, blocks)) & (
            lanes(rows, blocks) < live[:, t : t + 1]
        )
        count = jnp.sum(hit.astype(jnp.float32), axis=1, keepdims=True)
        table = jnp.where(query_tile == t, count, table)
    times[...] = table
    peak[...] = jnp.full(peak.shape, -jnp.inf, jnp.float32)

    turned_q, turned_v = wq[...].T, wv[...].T
    query = (dot(turned_q, window[own]) * head_dim ** (-0.5)).astype(jnp.bfloat16)
    head = sublanes(width, tok) // head_dim
    for h in range(HEADS):
        queries[h] = jnp.where(head == h, query, jnp.zeros_like(query))
    key_tile = lanes(width, tok) // TILE

    pl.semaphore_wait(barrier, len(peers))
    sends = []
    for n, (device, slot) in enumerate(peers):
        send = pltpu.make_async_remote_copy(
            src_ref=window.at[own],
            dst_ref=window.at[slot],
            send_sem=send_sem.at[n],
            recv_sem=recv_sem.at[slot],
            device_id=device,
            device_id_type=MESH,
        )
        send.start()
        sends.append(send)

    def gather(slot):
        x = window[slot]
        keys = dot(x.T, wk[...]).astype(jnp.bfloat16)
        value = dot(turned_v, x).astype(jnp.bfloat16)
        for j in range(tiles):
            values[slot, j] = jnp.where(key_tile == j, value, jnp.zeros_like(value))
        used = [times[pl.ds(slot * tiles + j, 1), :] > 0 for j in range(tiles)]
        for h in range(HEADS):
            s = dot(keys, queries[h])
            scores[slot, h] = s
            top = peak[h]
            for j in range(tiles):
                part = s[j * TILE : (j + 1) * TILE].reshape(TILE // 8, 8, tok).max(axis=0)
                top = jnp.maximum(top, jnp.where(used[j], part, -jnp.inf))
            peak[h] = top

    gather(own)

    def arrive(step, carry):
        turn = step // pieces
        which = jnp.where(turn == 0, 1, jnp.where(turn == 1, near, far))
        slot = which * pieces + lax.rem(quad + lax.rem(step, pieces), pieces)
        pltpu.make_async_copy(feat_ref, window.at[slot], recv_sem.at[slot]).wait()
        gather(slot)
        return carry

    lax.fori_loop(1, slots, arrive, 0)

    for h in range(HEADS):
        top = jnp.max(peak[h], axis=0, keepdims=True)
        total = jnp.zeros((8, tok), jnp.float32)
        summed = jnp.zeros((head_dim, tok), jnp.float32)
        span = slice(h * head_dim, (h + 1) * head_dim)
        for slot in range(slots):
            probs, often = [], []
            for j in range(tiles):
                u = slot * tiles + j
                many = times[u : u + 1, :]
                shift = jnp.where(many > 0, top, FAR)
                w = jnp.exp(scores[slot, h, j * TILE : (j + 1) * TILE] - shift)
                total = total + many * w.reshape(TILE // 8, 8, tok).sum(axis=0)
                probs.append(w.astype(jnp.bfloat16))
                often.append(many)
            left = jnp.concatenate([values[slot, j, span] for j in range(tiles)], axis=0)
            o = dot(left, jnp.concatenate(probs, axis=0))
            for j in range(tiles):
                summed = summed + often[j] * o[j * head_dim : (j + 1) * head_dim]
        total = jnp.sum(total, axis=0, keepdims=True)
        attended[span, :] = (summed / total).astype(jnp.bfloat16)
    out_ref[...] = dot(wo[...].T, attended[...]).astype(jnp.bfloat16)
    for send in sends:
        send.wait_send()


def body(
    features, w_query, w_key, w_value, w_out, block_offset, block_quad, block_tile, live_blocks
):
    tok, width = features.shape[1:]
    tiles = tok // TILE
    pieces, frames = lax.axis_size("quad"), lax.axis_size("tm")
    stride = frames // LOOP
    slots = 3 * pieces
    rows = -(-slots * tiles // 8) * 8
    listed = block_offset.shape
    hbm = pl.BlockSpec(memory_space=pltpu.HBM)
    vmem = pl.BlockSpec(memory_space=pltpu.VMEM)
    weights = pltpu.VMEM((width, width), jnp.bfloat16)
    mixed = pl.pallas_call(
        functools.partial(kernel, pieces, frames, stride),
        out_shape=jax.ShapeDtypeStruct((width, tok), jnp.bfloat16),
        in_specs=[hbm] * 9,
        out_specs=vmem,
        scratch_shapes=[
            pltpu.VMEM((slots, width, tok), jnp.bfloat16),
            weights,
            weights,
            weights,
            weights,
            pltpu.VMEM((width, tok), jnp.bfloat16),
            pltpu.VMEM(listed, jnp.int32),
            pltpu.VMEM(listed, jnp.int32),
            pltpu.VMEM(listed, jnp.int32),
            pltpu.VMEM(live_blocks.shape, jnp.int32),
            pltpu.VMEM((HEADS, width, tok), jnp.bfloat16),
            pltpu.VMEM((rows, tok), jnp.float32),
            pltpu.VMEM((slots, HEADS, tok, tok), jnp.float32),
            pltpu.VMEM((HEADS, 8, tok), jnp.float32),
            pltpu.VMEM((slots, tiles, width, tok), jnp.bfloat16),
            pltpu.SemaphoreType.DMA((9,)),
            pltpu.SemaphoreType.DMA((slots - 1,)),
            pltpu.SemaphoreType.DMA((slots,)),
        ],
        compiler_params=pltpu.CompilerParams(
            collective_id=0, has_side_effects=True, vmem_limit_bytes=60 << 20
        ),
    )(features[0].T, w_query, w_key, w_value, w_out, block_offset, block_quad, block_tile, live_blocks)
    return mixed.T[None]


def solution(mesh):
    listed = P("tm", "quad", None)
    return jax.shard_map(
        body,
        mesh=mesh,
        in_specs=(listed, P(), P(), P(), P(), listed, listed, listed, P("tm", "quad")),
        out_specs=listed,
        check_vma=False,
    )
```

```python
import functools

import jax
import jax.numpy as jnp
from jax import lax
from jax.experimental import pallas as pl
from jax.experimental.pallas import tpu as pltpu
from jax.sharding import PartitionSpec as P

HEADS = 6
TILE = 128
LOOP = 16
FAR = 1e30
MESH = pl.DeviceIdType.MESH


def dot(a, b):
    return jnp.dot(a, b, preferred_element_type=jnp.float32)


def lanes(rows, columns):
    return lax.broadcasted_iota(jnp.int32, (rows, columns), 1)


def sublanes(rows, columns):
    return lax.broadcasted_iota(jnp.int32, (rows, columns), 0)


def kernel(
    pieces, frames, stride,
    feat_ref, wq_ref, wk_ref, wv_ref, wo_ref, offset_ref, quad_ref, tile_ref, live_ref,
    out_ref,
    window, wq, wk, wv, wo, attended, offset, quads, places, live,
    queries, times, scores, peak, values,
    load_sem, send_sem, recv_sem,
):
    width, tok = feat_ref.shape
    head_dim = width // HEADS
    tiles = tok // TILE
    slots = 3 * pieces
    frame, quad = lax.axis_index("tm"), lax.axis_index("quad")
    near, far = 2 - 2 * lax.rem(frame, 2), 2 * lax.rem(frame, 2)
    own = pieces + quad

    peers = []
    for rank, which in enumerate((far, 1, near)):
        for turn in range(pieces):
            if rank == 1 and turn == 0:
                continue
            there = lax.rem(frame + (which - 1) * stride + frames, frames)
            slot = (2 - which) * pieces + quad
            peers.append(({"tm": there, "quad": lax.rem(quad + turn, pieces)}, slot))

    barrier = pltpu.get_barrier_semaphore()
    for device, _ in peers:
        pl.semaphore_signal(barrier, inc=1, device_id=device, device_id_type=MESH)

    pairs = (
        (wq_ref, wq), (feat_ref, window.at[own]), (wk_ref, wk), (wv_ref, wv),
        (offset_ref, offset), (quad_ref, quads), (tile_ref, places), (live_ref, live),
        (wo_ref, wo),
    )
    loads = [
        pltpu.make_async_copy(source, target, load_sem.at[n])
        for n, (source, target) in enumerate(pairs)
    ]
    for load in loads:
        load.start()
    loads[1].wait()
    pl.semaphore_wait(barrier, len(peers))
    sends = []
    for n, (device, slot) in enumerate(peers):
        send = pltpu.make_async_remote_copy(
            src_ref=window.at[own],
            dst_ref=window.at[slot],
            send_sem=send_sem.at[n],
            recv_sem=recv_sem.at[slot],
            device_id=device,
            device_id_type=MESH,
        )
        send.start()
        sends.append(send)
    for load in loads[:1] + loads[2:]:
        load.wait()

    rows = times.shape[0]
    ids = offset[0] * (pieces * tiles) + quads[0] * tiles + places[0]
    blocks = ids.shape[1]
    query_tile = lanes(rows, tok) // TILE
    table = jnp.zeros((rows, tok), jnp.float32)
    for t in range(tiles):
        hit = (ids[t : t + 1] == sublanes(rows, blocks)) & (
            lanes(rows, blocks) < live[:, t : t + 1]
        )
        count = jnp.sum(hit.astype(jnp.float32), axis=1, keepdims=True)
        table = jnp.where(query_tile == t, count, table)
    times[...] = table
    peak[...] = jnp.full(peak.shape, -jnp.inf, jnp.float32)

    turned_q, turned_v = wq[...].T, wv[...].T
    query = (dot(turned_q, window[own]) * head_dim ** (-0.5)).astype(jnp.bfloat16)
    head = sublanes(width, tok) // head_dim
    for h in range(HEADS):
        queries[h] = jnp.where(head == h, query, jnp.zeros_like(query))
    key_tile = lanes(width, tok) // TILE

    def gather(slot):
        x = window[slot]
        keys = dot(x.T, wk[...]).astype(jnp.bfloat16)
        value = dot(turned_v, x).astype(jnp.bfloat16)
        for j in range(tiles):
            values[slot, j] = jnp.where(key_tile == j, value, jnp.zeros_like(value))
        used = [times[pl.ds(slot * tiles + j, 1), :] > 0 for j in range(tiles)]
        for h in range(HEADS):
            s = dot(keys, queries[h])
            scores[slot, h] = s
            top = peak[h]
            for j in range(tiles):
                part = s[j * TILE : (j + 1) * TILE].reshape(TILE // 8, 8, tok).max(axis=0)
                top = jnp.maximum(top, jnp.where(used[j], part, -jnp.inf))
            peak[h] = top

    gather(own)

    def arrive(step, carry):
        turn = step // pieces
        which = jnp.where(turn == 0, 1, jnp.where(turn == 1, near, far))
        slot = which * pieces + lax.rem(quad + lax.rem(step, pieces), pieces)
        pltpu.make_async_copy(feat_ref, window.at[slot], recv_sem.at[slot]).wait()
        gather(slot)
        return carry

    lax.fori_loop(1, slots, arrive, 0)

    for h in range(HEADS):
        top = jnp.max(peak[h], axis=0, keepdims=True)
        total = jnp.zeros((8, tok), jnp.float32)
        summed = jnp.zeros((head_dim, tok), jnp.float32)
        span = slice(h * head_dim, (h + 1) * head_dim)
        for slot in range(slots):
            probs, often = [], []
            for j in range(tiles):
                u = slot * tiles + j
                many = times[u : u + 1, :]
                shift = jnp.where(many > 0, top, FAR)
                w = jnp.exp(scores[slot, h, j * TILE : (j + 1) * TILE] - shift)
                total = total + many * w.reshape(TILE // 8, 8, tok).sum(axis=0)
                probs.append(w.astype(jnp.bfloat16))
                often.append(many)
            left = jnp.concatenate([values[slot, j, span] for j in range(tiles)], axis=0)
            o = dot(left, jnp.concatenate(probs, axis=0))
            for j in range(tiles):
                summed = summed + often[j] * o[j * head_dim : (j + 1) * head_dim]
        total = jnp.sum(total, axis=0, keepdims=True)
        attended[span, :] = (summed / total).astype(jnp.bfloat16)
    out_ref[...] = dot(wo[...].T, attended[...]).astype(jnp.bfloat16)
    for send in sends:
        send.wait_send()


def body(
    features, w_query, w_key, w_value, w_out, block_offset, block_quad, block_tile, live_blocks
):
    tok, width = features.shape[1:]
    tiles = tok // TILE
    pieces, frames = lax.axis_size("quad"), lax.axis_size("tm")
    stride = frames // LOOP
    slots = 3 * pieces
    rows = -(-slots * tiles // 8) * 8
    listed = block_offset.shape
    hbm = pl.BlockSpec(memory_space=pltpu.HBM)
    vmem = pl.BlockSpec(memory_space=pltpu.VMEM)
    weights = pltpu.VMEM((width, width), jnp.bfloat16)
    mixed = pl.pallas_call(
        functools.partial(kernel, pieces, frames, stride),
        out_shape=jax.ShapeDtypeStruct((width, tok), jnp.bfloat16),
        in_specs=[hbm] * 9,
        out_specs=vmem,
        scratch_shapes=[
            pltpu.VMEM((slots, width, tok), jnp.bfloat16),
            weights,
            weights,
            weights,
            weights,
            pltpu.VMEM((width, tok), jnp.bfloat16),
            pltpu.VMEM(listed, jnp.int32),
            pltpu.VMEM(listed, jnp.int32),
            pltpu.VMEM(listed, jnp.int32),
            pltpu.VMEM(live_blocks.shape, jnp.int32),
            pltpu.VMEM((HEADS, width, tok), jnp.bfloat16),
            pltpu.VMEM((rows, tok), jnp.float32),
            pltpu.VMEM((slots, HEADS, tok, tok), jnp.float32),
            pltpu.VMEM((HEADS, 8, tok), jnp.float32),
            pltpu.VMEM((slots, tiles, width, tok), jnp.bfloat16),
            pltpu.SemaphoreType.DMA((9,)),
            pltpu.SemaphoreType.DMA((slots - 1,)),
            pltpu.SemaphoreType.DMA((slots,)),
        ],
        compiler_params=pltpu.CompilerParams(
            collective_id=0, has_side_effects=True, vmem_limit_bytes=60 << 20
        ),
    )(features[0].T, w_query, w_key, w_value, w_out, block_offset, block_quad, block_tile, live_blocks)
    return mixed.T[None]


def solution(mesh):
    listed = P("tm", "quad", None)
    return jax.shard_map(
        body,
        mesh=mesh,
        in_specs=(listed, P(), P(), P(), P(), listed, listed, listed, P("tm", "quad")),
        out_specs=listed,
        check_vma=False,
    )
```
